32 devices in a mesh: grp: 2 (over x), ex: 16 (over z, y, core).
Axes of the slice: x: 2, y: 2, z: 4, core: 2. Of those that a mesh axis runs over, the one named last changes fastest.
Arguments:
- queries: bfloat16 [256, 4096], P(('grp', 'ex')), parts along dimension 0, may hold values from -6 to 6
- train_grads: bfloat16 [32768, 4096], P(('grp', 'ex')), parts along dimension 0
Outputs:
- scores: float32 [128, 32768], P(None, ('grp', 'ex')), parts along dimension 1
- best_scores: float32 [256, 8], P(('grp', 'ex')), parts along dimension 0
The draws below stay inside these ranges and needn't reach their ends.
There are 2 independent parts, one for each index of `grp`. The reference program is written for one: setup_inputs(seed, part) draws one part's arguments, and reference() takes and returns one part's arrays. A program takes and returns all parts, laid end to end along the dimension named above; each array names one. Nothing has to cross between parts.
All inputs are finite; a program needn't handle non-finite values.
Results may differ from the reference program's by a relative error of at most 0.0003.
Values may be sent and summed in bfloat16 or wider, within the bound.
A program may use at most 192 MiB of HBM per device.

```python
import jax
import jax.numpy as jnp
from jax import lax

K = 4096
TOPV = 8
NTRAIN = 16384
NQ = 128


def draw_train_grads(key, part):
    key = jax.random.fold_in(key, 11)
    k_main, k_rows, k_cols = jax.random.split(key, 3)
    row_scale = jnp.exp(jax.random.uniform(k_rows, (NTRAIN, 1), jnp.float32) * jnp.log(10.0))
    col_scale = jnp.exp(jax.random.uniform(k_cols, (1, K), jnp.float32) * jnp.log(10.0))
    base = jax.random.normal(k_main, (NTRAIN, K), jnp.float32)
    return (base * row_scale * col_scale * 0.2).astype(jnp.bfloat16)


def block_scale(rng, shape, cuts, least, largest):
    factor_of, own = 1.0, jax.random.fold_in(rng, 6)
    for dim, parts in cuts:
        draws = jnp.exp(jax.random.uniform(jax.random.fold_in(own, dim), (parts,), jnp.float32, least / len(cuts), largest / len(cuts)))
        factor_of = factor_of * jnp.repeat(draws, shape[dim] // parts).reshape([-1 if axis == dim else 1 for axis in range(len(shape))])
    return factor_of


def normal_values(own_key, dims, deviation, most, cuts=(), dtype=jnp.bfloat16):
    level = block_scale(own_key, dims, cuts, -0.22, 0.18) if cuts else 1.0
    values = jax.random.normal(own_key, dims, jnp.float32) * deviation * level
    return jnp.minimum(jnp.maximum(values, -most), most).astype(dtype)


def setup_inputs(seed: int = 0, part: int = 0) -> dict:
    key_of = jax.random.split(jax.random.key(seed), 3)
    part_splits = jax.random.split(jax.random.fold_in(key_of[2], part), 3)
    queries = normal_values(part_splits[0], (NQ, K), 1.0, 6.0, ((0, 16),))
    train_grads = draw_train_grads(jax.random.fold_in(jax.random.fold_in(key_of[2], part), 71), part)
    return {"queries": queries, "train_grads": train_grads}


def reference(queries, train_grads):
    squares = jnp.square(train_grads.astype(jnp.float32))
    scale = lax.rsqrt(lax.optimization_barrier(jnp.mean(squares, axis=1)) + 1e-06) / jnp.sqrt(jnp.float32(K))
    raw = lax.dot_general(queries, train_grads, (((1,), (1,)), ((), ())), preferred_element_type=jnp.float32)
    scores = raw * scale[None, :]
    best_scores = lax.top_k(scores, TOPV)[0]
    return (scores, best_scores)
```

```python
import functools

import jax
import jax.numpy as jnp
from jax import lax
from jax.experimental import pallas as pl
from jax.experimental.pallas import tpu as pltpu
from jax.sharding import PartitionSpec as P

TOPV = 8
LANES = 128
CHUNKS = 4
SORT8 = (
    (0, 1), (2, 3), (4, 5), (6, 7), (0, 2), (1, 3), (4, 6), (5, 7), (1, 2), (5, 6),
    (0, 4), (1, 5), (2, 6), (3, 7), (2, 4), (3, 5), (1, 2), (3, 4), (5, 6),
)
MERGE8 = (
    (0, 4), (1, 5), (2, 6), (3, 7), (0, 2), (1, 3), (4, 6), (5, 7), (0, 1), (2, 3), (4, 5), (6, 7),
)


def network(rows, pairs):
    rows = list(rows)
    for i, j in pairs:
        rows[i], rows[j] = jnp.maximum(rows[i], rows[j]), jnp.minimum(rows[i], rows[j])
    return rows


def merge(left, right):
    return network([jnp.maximum(left[i], right[TOPV - 1 - i]) for i in range(TOPV)], MERGE8)


def over_sublanes(best):
    for shift in (4, 2, 1):
        best = merge(best, [pltpu.roll(row, shift, 0) for row in best])
    place = lax.broadcasted_iota(jnp.int32, best[0].shape, 0)
    tile = best[0]
    for i in range(1, TOPV):
        tile = jnp.where(place == i, best[i], tile)
    return tile


def each(count, body):
    if count <= 16:
        for i in range(count):
            body(i)
    else:
        lax.fori_loop(0, count, lambda i, _: (body(i), None)[1], None)


def kernel(
    outer, inner, q_ref, t_ref, scores_ref, best_ref,
    qbuf, tbuf, squares, scale, acc, outbuf, tile, tiles, turned,
    t_sem, own_sem, out_sem, recv_sem, send_z, send_y, send_c, tile_send, tile_recv,
):
    ex = 2 * outer * inner
    own, width = q_ref.shape
    rows = t_ref.shape[0]
    nq = ex * own
    groups = nq // LANES
    kc = width // CHUNKS
    me = lax.axis_index("ex")
    core = lax.rem(me, 2)
    chip = me // 2
    a, b = chip // inner, lax.rem(chip, inner)

    def at(aa, bb, cc):
        return (aa * inner + bb) * 2 + cc

    def columns(k):
        return pl.ds(k * kc, kc)

    t_copies = []
    for k in range(CHUNKS):
        copy = pltpu.make_async_copy(t_ref.at[:, columns(k)], tbuf.at[k], t_sem.at[k])
        copy.start()
        t_copies.append(copy)
    own_copies = []
    for k in range(CHUNKS):
        copy = pltpu.make_async_copy(q_ref.at[:, columns(k)], qbuf.at[k, me], own_sem.at[k])
        copy.start()
        own_copies.append(copy)

    barrier = pltpu.get_barrier_semaphore()

    def greet(i):
        pl.semaphore_signal(
            barrier, inc=1, device_id={"ex": lax.rem(me + 1 + i, ex)},
            device_id_type=pl.DeviceIdType.MESH,
        )

    each(ex - 1, greet)
    pl.semaphore_wait(barrier, ex - 1)

    def remote(k, slot, target, send, src=None):
        return pltpu.make_async_remote_copy(
            src_ref=qbuf.at[k, slot] if src is None else src,
            dst_ref=qbuf.at[k, slot],
            send_sem=send,
            recv_sem=recv_sem.at[k, slot],
            device_id={"ex": target},
            device_id_type=pl.DeviceIdType.MESH,
        )

    def z_copy(k, i):
        aa = lax.rem(a + 1 + i, outer)
        return remote(k, me, at(aa, b, core), send_z.at[k, i], q_ref.at[:, columns(k)])

    def y_copy(k, i, j):
        aa, bb = lax.rem(a + i, outer), lax.rem(b + 1 + j, inner)
        src = q_ref.at[:, columns(k)] if isinstance(i, int) and i == 0 else None
        return remote(k, at(aa, b, core), at(a, bb, core), send_y.at[k, i, j], src)

    def c_copy(k, i, j):
        aa, bb = lax.rem(a + i, outer), lax.rem(b + j, inner)
        src = q_ref.at[:, columns(k)] if isinstance(i, int) and isinstance(j, int) and i == j == 0 else None
        return remote(k, at(aa, bb, core), at(a, b, 1 - core), send_c.at[k, i, j], src)

    def arrived(k, slot):
        remote(k, slot, me, own_sem.at[k]).wait_recv()

    for k in range(CHUNKS):
        each(outer - 1, lambda i: z_copy(k, i).start())
        each(inner - 1, lambda j: y_copy(k, 0, j).start())
        c_copy(k, 0, 0).start()

    def pass_z(k):
        def one(i):
            arrived(k, at(lax.rem(a + 1 + i, outer), b, core))
            each(inner - 1, lambda j: y_copy(k, i + 1, j).start())
            c_copy(k, i + 1, 0).start()
        each(outer - 1, one)

    def pass_y(k):
        def one(i):
            def two(j):
                arrived(k, at(lax.rem(a + i, outer), lax.rem(b + 1 + j, inner), core))
                c_copy(k, i, j + 1).start()
            each(inner - 1, two)
        each(outer, one)

    def pass_c(k):
        def one(i):
            each(inner, lambda j: arrived(k, at(lax.rem(a + i, outer), lax.rem(b + j, inner), 1 - core)))
        each(outer, one)
        own_copies[k].wait()

    def square(k):
        t_copies[k].wait()
        block = 64

        def one(r, _):
            here = pl.ds(pl.multiple_of(r * block, block), block)
            total = None
            for g in range(kc // LANES):
                x = tbuf[k, here, pl.ds(g * LANES, LANES)].astype(jnp.float32)
                total = x * x if total is None else total + x * x
            if k:
                total = total + squares[here, :]
            if k < CHUNKS - 1:
                squares[here, :] = total
            else:
                mean = jnp.sum(total, axis=1, keepdims=True) * jnp.float32(1.0 / width)
                factor = lax.rsqrt(mean + 1e-06) * jnp.float32(width ** -0.5)
                scale[here, :] = jnp.broadcast_to(factor, (block, LANES))

        lax.fori_loop(0, rows // block, one, None)

    def query_block(k, g):
        per = LANES // own
        return qbuf[k, pl.ds(g * per, per)].reshape(LANES, kc)

    def product(k, here, g):
        return lax.dot_general(
            tbuf[k, here, :], query_block(k, g), (((1,), (1,)), ((), ())),
            preferred_element_type=jnp.float32,
        )

    def multiply(k):
        def one(g):
            new = product(k, slice(None), g)
            acc[g] = new if k == 0 else acc[g] + new
        each(groups, one)

    step = 256
    out_copies = []

    def last(g):
        best = None
        for r in range(rows // step):
            here = pl.ds(r * step, step)
            value = (acc[g, here, :] + product(CHUNKS - 1, here, g)) * scale[here, :]
            for s in range(step // LANES):
                outbuf[pl.ds(g * LANES, LANES), pl.ds(r * step + s * LANES, LANES)] = (
                    value[s * LANES:(s + 1) * LANES].T
                )
            for s in range(step // 64):
                lists = network([value[s * 64 + i * 8:s * 64 + i * 8 + 8] for i in range(8)], SORT8)
                best = lists if best is None else merge(best, lists)
        tile[g] = over_sublanes(best)

    for t in range(CHUNKS + 2):
        if t < CHUNKS:
            pass_z(t)
        if 0 <= t - 1 < CHUNKS:
            pass_y(t - 1)
        if t < CHUNKS:
            square(t)
        k = t - 2
        if 0 <= k < CHUNKS:
            pass_c(k)
            if k < CHUNKS - 1:
                multiply(k)
            else:
                each(groups, last)

    def tile_copy(i):
        target = lax.rem(me + 1 + i, ex)
        return pltpu.make_async_remote_copy(
            src_ref=tile.at[target * own // LANES],
            dst_ref=tiles.at[me],
            send_sem=tile_send.at[i],
            recv_sem=tile_recv.at[me],
            device_id={"ex": target},
            device_id_type=pl.DeviceIdType.MESH,
        )

    each(ex - 1, lambda i: tile_copy(i).start())
    out = pltpu.make_async_copy(outbuf, scores_ref, out_sem)
    out.start()
    tiles[me] = tile[me * own // LANES]

    def tile_wait(i):
        source = lax.rem(me + 1 + i, ex)
        pltpu.make_async_remote_copy(
            src_ref=tile.at[0], dst_ref=tiles.at[source], send_sem=tile_send.at[i],
            recv_sem=tile_recv.at[source], device_id={"ex": source},
            device_id_type=pl.DeviceIdType.MESH,
        ).wait_recv()

    each(ex - 1, tile_wait)
    best = None
    for s in range(ex // 8):
        lists = network([tiles[s * 8 + i] for i in range(8)], SORT8)
        best = lists if best is None else merge(best, lists)
    turned[...] = over_sublanes(best).T
    best_ref[...] = turned[pl.ds(pl.multiple_of(lax.rem(me * own, LANES), own), own), :]

    each(ex - 1, lambda i: tile_copy(i).wait_send())
    for k in range(CHUNKS):
        each(outer - 1, lambda i: z_copy(k, i).wait_send())
        each(outer, lambda i: each(inner - 1, lambda j: y_copy(k, i, j).wait_send()))
        each(outer, lambda i: each(inner, lambda j: c_copy(k, i, j).wait_send()))
    out.wait()


def shards(ex, queries, train_grads):
    own, width = queries.shape
    rows = train_grads.shape[0]
    nq = ex * own
    groups = nq // LANES
    kc = width // CHUNKS
    chips = ex // 2
    inner = 1
    while inner * inner * 4 <= chips:
        inner *= 2
    outer = chips // inner
    any_space = pl.BlockSpec(memory_space=pl.ANY)
    dma = pltpu.SemaphoreType.DMA
    return pl.pallas_call(
        functools.partial(kernel, outer, inner),
        out_shape=(
            jax.ShapeDtypeStruct((nq, rows), jnp.float32),
            jax.ShapeDtypeStruct((own, TOPV), jnp.float32),
        ),
        in_specs=[any_space, any_space],
        out_specs=(any_space, pl.BlockSpec(memory_space=pltpu.VMEM)),
        scratch_shapes=[
            pltpu.VMEM((CHUNKS, ex, own, kc), jnp.bfloat16),
            pltpu.VMEM((CHUNKS, rows, kc), jnp.bfloat16),
            pltpu.VMEM((rows, LANES), jnp.float32),
            pltpu.VMEM((rows, LANES), jnp.float32),
            pltpu.VMEM((groups, rows, LANES), jnp.float32),
            pltpu.VMEM((nq, rows), jnp.float32),
            pltpu.VMEM((groups, TOPV, LANES), jnp.float32),
            pltpu.VMEM((ex, TOPV, LANES), jnp.float32),
            pltpu.VMEM((LANES, TOPV), jnp.float32),
            dma((CHUNKS,)),
            dma((CHUNKS,)),
            dma,
            dma((CHUNKS, ex)),
            dma((CHUNKS, max(outer - 1, 1))),
            dma((CHUNKS, outer, max(inner - 1, 1))),
            dma((CHUNKS, outer, inner)),
            dma((ex,)),
            dma((ex,)),
        ],
        compiler_params=pltpu.CompilerParams(
            collective_id=0, has_side_effects=True, vmem_limit_bytes=48 * 1024 * 1024
        ),
    )(queries, train_grads)


def solution(mesh):
    in_specs = (P(("grp", "ex"), None), P(("grp", "ex"), None))
    out_specs = (P(None, ("grp", "ex")), P(("grp", "ex"), None))
    return jax.shard_map(
        functools.partial(shards, mesh.shape["ex"]),
        mesh=mesh, in_specs=in_specs, out_specs=out_specs, check_vma=False,
    )
```

```python
import functools

import jax
import jax.numpy as jnp
from jax import lax
from jax.experimental import pallas as pl
from jax.experimental.pallas import tpu as pltpu
from jax.sharding import PartitionSpec as P

TOPV = 8
LANES = 128
SHARES = (1, 1)
PER_EVENT = 4
VMEM_MIB = 48
SORT8 = (
    (0, 1), (2, 3), (4, 5), (6, 7), (0, 2), (1, 3), (4, 6), (5, 7), (1, 2), (5, 6),
    (0, 4), (1, 5), (2, 6), (3, 7), (2, 4), (3, 5), (1, 2), (3, 4), (5, 6),
)
MERGE8 = (
    (0, 4), (1, 5), (2, 6), (3, 7), (0, 2), (1, 3), (4, 6), (5, 7), (0, 1), (2, 3), (4, 5), (6, 7),
)


def network(rows, pairs):
    rows = list(rows)
    for i, j in pairs:
        rows[i], rows[j] = jnp.maximum(rows[i], rows[j]), jnp.minimum(rows[i], rows[j])
    return rows


def merge(left, right):
    return network([jnp.maximum(left[i], right[TOPV - 1 - i]) for i in range(TOPV)], MERGE8)


def over_sublanes(best):
    for shift in (4, 2, 1):
        best = merge(best, [pltpu.roll(row, shift, 0) for row in best])
    place = lax.broadcasted_iota(jnp.int32, best[0].shape, 0)
    tile = best[0]
    for i in range(1, TOPV):
        tile = jnp.where(place == i, best[i], tile)
    return tile


def each(count, body):
    if count <= 16:
        for i in range(count):
            body(i)
    else:
        lax.fori_loop(0, count, lambda i, _: (body(i), None)[1], None)


def kernel(outer, inner, widths, q_ref, t_ref, scores_ref, best_ref, *scratch):
    chunks = len(widths)
    qbufs, tbufs = scratch[:chunks], scratch[chunks:2 * chunks]
    (
        squares, scale, acc, tile, tiles, turned, t_sem, own_sem,
        z_send, z_recv, y_send, y_recv, c_send, c_recv, tile_send, tile_recv,
    ) = scratch[2 * chunks:]
    ex = 2 * outer * inner
    own, width = q_ref.shape
    rows = t_ref.shape[0]
    groups = ex * own // LANES
    starts = [sum(widths[:k]) for k in range(chunks)]
    me = lax.axis_index("ex")
    core = lax.rem(me, 2)
    chip = me // 2
    a, b = chip // inner, lax.rem(chip, inner)

    def at(aa, bb, cc):
        return (aa * inner + bb) * 2 + cc

    def own_block(k):
        return q_ref.at[:, pl.ds(starts[k], widths[k])]

    barrier = pltpu.get_barrier_semaphore()

    def greet(i):
        pl.semaphore_signal(
            barrier, inc=1, device_id={"ex": lax.rem(me + 1 + i, ex)},
            device_id_type=pl.DeviceIdType.MESH,
        )

    each(ex - 1, greet)
    t_copies = []
    for k in range(chunks):
        copy = pltpu.make_async_copy(t_ref.at[:, pl.ds(starts[k], widths[k])], tbufs[k], t_sem.at[k])
        copy.start()
        t_copies.append(copy)
    own_copies = []
    for k in range(chunks):
        copy = pltpu.make_async_copy(own_block(k), qbufs[k].at[core, b, a], own_sem.at[k])
        copy.start()
        own_copies.append(copy)
    pl.semaphore_wait(barrier, ex - 1)

    def remote(src, dst, send, recv, target):
        return pltpu.make_async_remote_copy(
            src_ref=src, dst_ref=dst, send_sem=send, recv_sem=recv,
            device_id={"ex": target}, device_id_type=pl.DeviceIdType.MESH,
        )

    def z_copy(k, i):
        target = at(lax.rem(a + 1 + i, outer), b, core)
        return remote(own_block(k), qbufs[k].at[core, b, a], z_send.at[k, i], z_recv.at[k, a], target)

    def y_copy(k, i, j):
        aa, bb = lax.rem(a + i, outer), lax.rem(b + 1 + j, inner)
        place = qbufs[k].at[core, b, aa]
        src = own_block(k) if isinstance(i, int) and i == 0 else place
        return remote(src, place, y_send.at[k, j, i], y_recv.at[k, b, aa], at(a, bb, core))

    def c_copy(k, j):
        bb = lax.rem(b + j, inner)
        place = qbufs[k].at[core, bb]
        return remote(place, place, c_send.at[k, j], c_recv.at[k, bb], at(a, b, 1 - core))

    def arrived(place, sem):
        remote(place, place, sem, sem, me).wait_recv()

    for k in range(chunks):
        each(outer - 1, lambda i: z_copy(k, i).start())
        each(inner - 1, lambda j: y_copy(k, 0, j).start())

    def pass_z(k):
        def one(i):
            aa = lax.rem(a + 1 + i, outer)
            arrived(qbufs[k].at[core, b, aa], z_recv.at[k, aa])
            each(inner - 1, lambda j: y_copy(k, i + 1, j).start())
        each(outer - 1, one)
        own_copies[k].wait()
        c_copy(k, 0).start()

    def pass_y(k):
        def two(j):
            bb = lax.rem(b + 1 + j, inner)
            each(outer, lambda aa: arrived(qbufs[k].at[core, bb, aa], y_recv.at[k, bb, aa]))
            c_copy(k, j + 1).start()
        each(inner - 1, two)

    def pass_c(k):
        each(inner, lambda bb: arrived(qbufs[k].at[1 - core, bb], c_recv.at[k, bb]))

    parts = 4
    block = 64

    def square(k, part):
        if part == 0:
            t_copies[k].wait()
        count = rows // block // parts

        def one(r, _):
            here = pl.ds(pl.multiple_of(r * block, block), block)
            total = None
            for g in range(widths[k] // LANES):
                x = tbufs[k][here, pl.ds(g * LANES, LANES)].astype(jnp.float32)
                total = x * x if total is None else total + x * x
            if k:
                total = total + squares[here, :]
            if k < chunks - 1:
                squares[here, :] = total
            else:
                mean = jnp.sum(total, axis=1, keepdims=True) * jnp.float32(1.0 / width)
                factor = lax.rsqrt(mean + 1e-06) * jnp.float32(width ** -0.5)
                scale[here, :] = jnp.broadcast_to(factor, (block, LANES))

        lax.fori_loop(part * count, (part + 1) * count, one, None)

    def query_block(k, g):
        per = LANES // own
        blocks = [qbufs[k][e % 2, e // 2 % inner, e // 2 // inner] for e in range(g * per, (g + 1) * per)]
        return jnp.concatenate(blocks, axis=0)

    def product(k, here, g):
        return lax.dot_general(
            tbufs[k][here, :], query_block(k, g), (((1,), (1,)), ((), ())),
            preferred_element_type=jnp.float32,
        )

    def multiply(k, part):
        half = rows // 2
        here = pl.ds(part * half, half)

        def one(g):
            new = product(k, here, g)
            acc[g, here, :] = new if k == 0 else acc[g, here, :] + new
        each(groups, one)

    step = 256

    def last(g):
        best = None
        for r in range(rows // step):
            here = pl.ds(r * step, step)
            value = (acc[g, here, :] + product(chunks - 1, here, g)) * scale[here, :]
            for s in range(step // LANES):
                scores_ref[pl.ds(g * LANES, LANES), pl.ds(r * step + s * LANES, LANES)] = (
                    value[s * LANES:(s + 1) * LANES].T
                )
            for s in range(step // 64):
                lists = network([value[s * 64 + i * 8:s * 64 + i * 8 + 8] for i in range(8)], SORT8)
                best = lists if best is None else merge(best, lists)
        tile[g] = over_sublanes(best)

    events = []
    for t in range(chunks + 2):
        events += [(pass_z, t)] * (t < chunks) + [(pass_y, t - 1)] * (0 <= t - 1 < chunks)
        events += [(pass_c, t - 2)] * (0 <= t - 2)
    pending = [(square, k, part) for k in range(chunks) for part in range(parts)]
    for event, k in events:
        event(k)
        if event is pass_c and k < chunks - 1:
            pending += [(multiply, k, 0), (multiply, k, 1)]
        for work, *which in pending[:PER_EVENT]:
            work(*which)
        del pending[:PER_EVENT]
    for work, *which in pending:
        work(*which)
    each(groups, last)

    def tile_copy(i):
        target = lax.rem(me + 1 + i, ex)
        return remote(tile.at[target * own // LANES], tiles.at[me], tile_send.at[i], tile_recv.at[me], target)

    each(ex - 1, lambda i: tile_copy(i).start())
    tiles[me] = tile[me * own // LANES]

    def tile_wait(i):
        source = lax.rem(me + 1 + i, ex)
        arrived(tiles.at[source], tile_recv.at[source])

    each(ex - 1, tile_wait)
    best = None
    for s in range(ex // 8):
        lists = network([tiles[s * 8 + i] for i in range(8)], SORT8)
        best = lists if best is None else merge(best, lists)
    turned[...] = over_sublanes(best).T
    best_ref[...] = turned[pl.ds(pl.multiple_of(lax.rem(me * own, LANES), own), own), :]

    each(ex - 1, lambda i: tile_copy(i).wait_send())
    for k in range(chunks):
        each(outer - 1, lambda i: z_copy(k, i).wait_send())
        each(outer, lambda i: each(inner - 1, lambda j: y_copy(k, i, j).wait_send()))
        each(inner, lambda j: c_copy(k, j).wait_send())


def shards(ex, queries, train_grads):
    own, width = queries.shape
    rows = train_grads.shape[0]
    nq = ex * own
    groups = nq // LANES
    widths = [width * part // sum(SHARES) for part in SHARES]
    chunks = len(widths)
    chips = ex // 2
    inner = 1
    while inner * inner * 4 <= chips:
        inner *= 2
    outer = chips // inner
    any_space = pl.BlockSpec(memory_space=pl.ANY)
    vmem = pl.BlockSpec(memory_space=pltpu.VMEM)
    dma = pltpu.SemaphoreType.DMA
    return pl.pallas_call(
        functools.partial(kernel, outer, inner, widths),
        out_shape=(
            jax.ShapeDtypeStruct((nq, rows), jnp.float32),
            jax.ShapeDtypeStruct((own, TOPV), jnp.float32),
        ),
        in_specs=[any_space, any_space],
        out_specs=(vmem, vmem),
        scratch_shapes=[
            *[pltpu.VMEM((2, inner, outer, own, kc), jnp.bfloat16) for kc in widths],
            *[pltpu.VMEM((rows, kc), jnp.bfloat16) for kc in widths],
            pltpu.VMEM((rows, LANES), jnp.float32),
            pltpu.VMEM((rows, LANES), jnp.float32),
            pltpu.VMEM((groups, rows, LANES), jnp.float32),
            pltpu.VMEM((groups, TOPV, LANES), jnp.float32),
            pltpu.VMEM((ex, TOPV, LANES), jnp.float32),
            pltpu.VMEM((LANES, TOPV), jnp.float32),
            dma((chunks,)),
            dma((chunks,)),
            dma((chunks, max(outer - 1, 1))),
            dma((chunks, outer)),
            dma((chunks, max(inner - 1, 1), outer)),
            dma((chunks, inner, outer)),
            dma((chunks, inner)),
            dma((chunks, inner)),
            dma((ex,)),
            dma((ex,)),
        ],
        compiler_params=pltpu.CompilerParams(
            collective_id=0, has_side_effects=True, vmem_limit_bytes=VMEM_MIB * 1024 * 1024
        ),
    )(queries, train_grads)


def solution(mesh):
    in_specs = (P(("grp", "ex"), None), P(("grp", "ex"), None))
    out_specs = (P(None, ("grp", "ex")), P(("grp", "ex"), None))
    return jax.shard_map(
        functools.partial(shards, mesh.shape["ex"]),
        mesh=mesh, in_specs=in_specs, out_specs=out_specs, check_vma=False,
    )
```

```python
import functools

import jax
import jax.numpy as jnp
from jax import lax
from jax.experimental import pallas as pl
from jax.experimental.pallas import tpu as pltpu
from jax.sharding import PartitionSpec as P

TOPV = 8
LANES = 128
SHARES = (1, 1)
PER_EVENT = 4
VMEM_MIB = 48
SORT8 = (
    (0, 1), (2, 3), (4, 5), (6, 7), (0, 2), (1, 3), (4, 6), (5, 7), (1, 2), (5, 6),
    (0, 4), (1, 5), (2, 6), (3, 7), (2, 4), (3, 5), (1, 2), (3, 4), (5, 6),
)
MERGE8 = (
    (0, 4), (1, 5), (2, 6), (3, 7), (0, 2), (1, 3), (4, 6), (5, 7), (0, 1), (2, 3), (4, 5), (6, 7),
)


def network(rows, pairs):
    rows = list(rows)
    for i, j in pairs:
        rows[i], rows[j] = jnp.maximum(rows[i], rows[j]), jnp.minimum(rows[i], rows[j])
    return rows


def merge(left, right):
    return network([jnp.maximum(left[i], right[TOPV - 1 - i]) for i in range(TOPV)], MERGE8)


def over_sublanes(best):
    for shift in (4, 2, 1):
        best = merge(best, [pltpu.roll(row, shift, 0) for row in best])
    place = lax.broadcasted_iota(jnp.int32, best[0].shape, 0)
    tile = best[0]
    for i in range(1, TOPV):
        tile = jnp.where(place == i, best[i], tile)
    return tile


def each(count, body):
    if count <= 16:
        for i in range(count):
            body(i)
    else:
        lax.fori_loop(0, count, lambda i, _: (body(i), None)[1], None)


def kernel(outer, inner, widths, q_ref, t_ref, scores_ref, best_ref, *scratch):
    chunks = len(widths)
    qbufs, tbufs = scratch[:chunks], scratch[chunks:2 * chunks]
    (
        squares, scale, acc, tile, tiles, turned, t_sem, own_sem,
        z_send, z_recv, y_send, y_recv, c_send, c_recv, tile_send, tile_recv,
    ) = scratch[2 * chunks:]
    ex = 2 * outer * inner
    own, width = q_ref.shape
    rows = t_ref.shape[0]
    groups = ex * own // LANES
    starts = [sum(widths[:k]) for k in range(chunks)]
    me = lax.axis_index("ex")
    core = lax.rem(me, 2)
    chip = me // 2
    a, b = chip // inner, lax.rem(chip, inner)

    def at(aa, bb, cc):
        return (aa * inner + bb) * 2 + cc

    def own_block(k):
        return q_ref.at[:, pl.ds(starts[k], widths[k])]

    barrier = pltpu.get_barrier_semaphore()

    def greet(target):
        pl.semaphore_signal(
            barrier, inc=1, device_id={"ex": target}, device_id_type=pl.DeviceIdType.MESH
        )

    each(outer - 1, lambda i: greet(at(lax.rem(a + 1 + i, outer), b, core)))
    each(inner - 1, lambda j: greet(at(a, lax.rem(b + 1 + j, inner), core)))
    greet(at(a, b, 1 - core))
    t_copies = []
    for k in range(chunks):
        copy = pltpu.make_async_copy(t_ref.at[:, pl.ds(starts[k], widths[k])], tbufs[k], t_sem.at[k])
        copy.start()
        t_copies.append(copy)
    own_copies = []
    for k in range(chunks):
        copy = pltpu.make_async_copy(own_block(k), qbufs[k].at[core, b, a], own_sem.at[k])
        copy.start()
        own_copies.append(copy)
    pl.semaphore_wait(barrier, outer + inner - 1)

    def remote(src, dst, send, recv, target):
        return pltpu.make_async_remote_copy(
            src_ref=src, dst_ref=dst, send_sem=send, recv_sem=recv,
            device_id={"ex": target}, device_id_type=pl.DeviceIdType.MESH,
        )

    def z_copy(k, i):
        target = at(lax.rem(a + 1 + i, outer), b, core)
        return remote(own_block(k), qbufs[k].at[core, b, a], z_send.at[k, i], z_recv.at[k, a], target)

    def y_copy(k, i, j):
        aa, bb = lax.rem(a + i, outer), lax.rem(b + 1 + j, inner)
        place = qbufs[k].at[core, b, aa]
        src = own_block(k) if isinstance(i, int) and i == 0 else place
        return remote(src, place, y_send.at[k, j, i], y_recv.at[k, b, aa], at(a, bb, core))

    def c_copy(k, j):
        bb = lax.rem(b + j, inner)
        place = qbufs[k].at[core, bb]
        return remote(place, place, c_send.at[k, j], c_recv.at[k, bb], at(a, b, 1 - core))

    def arrived(place, sem):
        remote(place, place, sem, sem, me).wait_recv()

    for k in range(chunks):
        each(outer - 1, lambda i: z_copy(k, i).start())
        each(inner - 1, lambda j: y_copy(k, 0, j).start())

    def pass_z(k):
        def one(i):
            aa = lax.rem(a + 1 + i, outer)
            arrived(qbufs[k].at[core, b, aa], z_recv.at[k, aa])
            each(inner - 1, lambda j: y_copy(k, i + 1, j).start())
        each(outer - 1, one)
        own_copies[k].wait()
        c_copy(k, 0).start()

    def pass_y(k):
        def two(j):
            bb = lax.rem(b + 1 + j, inner)
            each(outer, lambda aa: arrived(qbufs[k].at[core, bb, aa], y_recv.at[k, bb, aa]))
            c_copy(k, j + 1).start()
        each(inner - 1, two)

    def pass_c(k):
        each(inner, lambda bb: arrived(qbufs[k].at[1 - core, bb], c_recv.at[k, bb]))

    parts = 4
    block = 64

    def square(k, part):
        if part == 0:
            t_copies[k].wait()
        count = rows // block // parts

        def one(r, _):
            here = pl.ds(pl.multiple_of(r * block, block), block)
            total = None
            for g in range(widths[k] // LANES):
                x = tbufs[k][here, pl.ds(g * LANES, LANES)].astype(jnp.float32)
                total = x * x if total is None else total + x * x
            if k:
                total = total + squares[here, :]
            if k < chunks - 1:
                squares[here, :] = total
            else:
                mean = jnp.sum(total, axis=1, keepdims=True) * jnp.float32(1.0 / width)
                factor = lax.rsqrt(mean + 1e-06) * jnp.float32(width ** -0.5)
                scale[here, :] = jnp.broadcast_to(factor, (block, LANES))

        lax.fori_loop(part * count, (part + 1) * count, one, None)

    def query_block(k, g):
        per = LANES // own
        blocks = [qbufs[k][e % 2, e // 2 % inner, e // 2 // inner] for e in range(g * per, (g + 1) * per)]
        return jnp.concatenate(blocks, axis=0)

    def product(k, here, g):
        return lax.dot_general(
            tbufs[k][here, :], query_block(k, g), (((1,), (1,)), ((), ())),
            preferred_element_type=jnp.float32,
        )

    def multiply(k, part):
        half = rows // 2
        here = pl.ds(part * half, half)

        def one(g):
            new = product(k, here, g)
            acc[g, here, :] = new if k == 0 else acc[g, here, :] + new
        each(groups, one)

    step = 256

    def last(g):
        best = None
        for r in range(rows // step):
            here = pl.ds(r * step, step)
            value = (acc[g, here, :] + product(chunks - 1, here, g)) * scale[here, :]
            for s in range(step // LANES):
                scores_ref[pl.ds(g * LANES, LANES), pl.ds(r * step + s * LANES, LANES)] = (
                    value[s * LANES:(s + 1) * LANES].T
                )
            for s in range(step // 64):
                lists = network([value[s * 64 + i * 8:s * 64 + i * 8 + 8] for i in range(8)], SORT8)
                best = lists if best is None else merge(best, lists)
        tile[g] = over_sublanes(best)

    events = []
    for t in range(chunks + 2):
        events += [(pass_z, t)] * (t < chunks) + [(pass_y, t - 1)] * (0 <= t - 1 < chunks)
        events += [(pass_c, t - 2)] * (0 <= t - 2)
    pending = [(square, k, part) for k in range(chunks) for part in range(parts)]
    for event, k in events:
        event(k)
        if event is pass_c and k < chunks - 1:
            pending += [(multiply, k, 0), (multiply, k, 1)]
        for work, *which in pending[:PER_EVENT]:
            work(*which)
        del pending[:PER_EVENT]
    for work, *which in pending:
        work(*which)
    each(groups, last)

    def tile_copy(i):
        target = lax.rem(me + 1 + i, ex)
        return remote(tile.at[target * own // LANES], tiles.at[me], tile_send.at[i], tile_recv.at[me], target)

    each(ex - 1, lambda i: tile_copy(i).start())
    tiles[me] = tile[me * own // LANES]

    def tile_wait(i):
        source = lax.rem(me + 1 + i, ex)
        arrived(tiles.at[source], tile_recv.at[source])

    each(ex - 1, tile_wait)
    best = None
    for s in range(ex // 8):
        lists = network([tiles[s * 8 + i] for i in range(8)], SORT8)
        best = lists if best is None else merge(best, lists)
    turned[...] = over_sublanes(best).T
    best_ref[...] = turned[pl.ds(pl.multiple_of(lax.rem(me * own, LANES), own), own), :]

    each(ex - 1, lambda i: tile_copy(i).wait_send())
    for k in range(chunks):
        each(outer - 1, lambda i: z_copy(k, i).wait_send())
        each(outer, lambda i: each(inner - 1, lambda j: y_copy(k, i, j).wait_send()))
        each(inner, lambda j: c_copy(k, j).wait_send())


def shards(ex, queries, train_grads):
    own, width = queries.shape
    rows = train_grads.shape[0]
    nq = ex * own
    groups = nq // LANES
    widths = [width * part // sum(SHARES) for part in SHARES]
    chunks = len(widths)
    chips = ex // 2
    inner = 1
    while inner * inner * 4 <= chips:
        inner *= 2
    outer = chips // inner
    any_space = pl.BlockSpec(memory_space=pl.ANY)
    vmem = pl.BlockSpec(memory_space=pltpu.VMEM)
    dma = pltpu.SemaphoreType.DMA
    return pl.pallas_call(
        functools.partial(kernel, outer, inner, widths),
        out_shape=(
            jax.ShapeDtypeStruct((nq, rows), jnp.float32),
            jax.ShapeDtypeStruct((own, TOPV), jnp.float32),
        ),
        in_specs=[any_space, any_space],
        out_specs=(vmem, vmem),
        scratch_shapes=[
            *[pltpu.VMEM((2, inner, outer, own, kc), jnp.bfloat16) for kc in widths],
            *[pltpu.VMEM((rows, kc), jnp.bfloat16) for kc in widths],
            pltpu.VMEM((rows, LANES), jnp.float32),
            pltpu.VMEM((rows, LANES), jnp.float32),
            pltpu.VMEM((groups, rows, LANES), jnp.float32),
            pltpu.VMEM((groups, TOPV, LANES), jnp.float32),
            pltpu.VMEM((ex, TOPV, LANES), jnp.float32),
            pltpu.VMEM((LANES, TOPV), jnp.float32),
            dma((chunks,)),
            dma((chunks,)),
            dma((chunks, max(outer - 1, 1))),
            dma((chunks, outer)),
            dma((chunks, max(inner - 1, 1), outer)),
            dma((chunks, inner, outer)),
            dma((chunks, inner)),
            dma((chunks, inner)),
            dma((ex,)),
            dma((ex,)),
        ],
        compiler_params=pltpu.CompilerParams(
            collective_id=0, has_side_effects=True, vmem_limit_bytes=VMEM_MIB * 1024 * 1024
        ),
    )(queries, train_grads)


def solution(mesh):
    in_specs = (P(("grp", "ex"), None), P(("grp", "ex"), None))
    out_specs = (P(None, ("grp", "ex")), P(("grp", "ex"), None))
    return jax.shard_map(
        functools.partial(shards, mesh.shape["ex"]),
        mesh=mesh, in_specs=in_specs, out_specs=out_specs, check_vma=False,
    )
```
